512 devices in a mesh: row: 64 (over z_hi, y, x, core), col: 8 (over z_lo).
Axes of the slice: x: 4, y: 4, z: 16 (z_hi: 2, z_lo: 8; z = z_hi * 8 + z_lo), core: 2. Of those that a mesh axis runs over, the one named last changes fastest.
Arguments:
- air_state: bfloat16 [65536, 384], P(('row', 'col')), may hold values from -6 to 6
- owner_map: int32 [65536, 1], P(('row', 'col')), may hold values from 0 to 63; in each aligned block of 128 rows (0 to 127, 128 to 255, ...) at most 4 rows name the same one
- cost_class: int32 [65536], P(('row', 'col')), may hold values from 0 to 3
- connectivity: int32 [4, 65536], P(None, ('row', 'col')), may hold values from -32 to 32, as said below
- inverse_blocks: bfloat16 [512, 4, 3, 128, 128], P(('row', 'col')), may hold values from -0.5 to 0.5
Outputs:
- new_state: bfloat16 [65536, 384], P(('row', 'col'))
The draws below stay inside these ranges and needn't reach their ends.
Inputs may be any that keep to these rules, and one draw needn't show every extreme that they name: `owner_map`: among the columns of one device no owner row is named by more than 4 columns, and some owner row is named by exactly 4. `connectivity`: offsets are never zero; both ends of the range occur.
All inputs are finite; a program needn't handle non-finite values.
Results may differ from the reference program's by a relative error of at most 0.0037.
Values may be sent and summed in bfloat16 or wider, within the bound.
A program may use at most 128 MiB of HBM per device.

```python
import math
import jax
import jax.numpy as jnp
import numpy as np
from jax import lax

LEV = 128
NCLASS = 4
PARTNERS = 4
COLS_DEV = 128
FEAT = 384
EDGE = 32
CAP = 4
GROUP_COLS = 1024
OWNERS = 512
COLUMNS = 65536
N_ROW = 64
N_COL = 8


def draw_connectivity(key, part):
    size_key, sign_key = jax.random.split(key)
    magnitude = jax.random.randint(size_key, (PARTNERS, COLUMNS), 1, EDGE + 1)
    sign_draw = jax.random.randint(sign_key, (PARTNERS, COLUMNS), 0, 2) * 2 - 1
    offsets = (magnitude * sign_draw).astype(jnp.int32)
    return offsets.at[0, 0].set(EDGE).at[1, 0].set(-EDGE)


def set_ends(entries, own_key, least, top_value):
    index_at = [jax.random.randint(jax.random.fold_in(own_key, axis), (), 0, length) for axis, length in enumerate(entries.shape)]
    widest = entries.shape.index(max(entries.shape))
    next_to = index_at[:widest] + [(index_at[widest] + 1) % entries.shape[widest]] + index_at[widest + 1:]
    return entries.at[tuple(index_at)].set(least).at[tuple(next_to)].set(top_value)


def block_scale(key, dims, cuts, low, largest):
    gain = 1.0
    for dim, blocks in cuts:
        steps = jax.random.uniform(jax.random.fold_in(jax.random.fold_in(key, 6), dim), (blocks,), jnp.float32, low / len(cuts), largest / len(cuts))
        gain = gain * jnp.repeat(jnp.exp(steps), dims[dim] // blocks).reshape((-1,) + (1,) * (len(dims) - 1 - dim))
    return gain


def shared_out(own_key, own, number, rows, count, top, limit, lean):
    ranking = jax.random.permutation(own_key, count)
    crowded, common = portions_of(count, rows * top, limit, lean, True), portions_of(count, rows * top, limit, lean, False)
    places = jnp.arange(count)

    def named(lengths, rotation):
        used = int((lengths > 0).sum())
        fixed = max(1, used // 4)
        passed = fixed + (places - fixed + rotation * (used - fixed)) % max(1, count - fixed)
        return jnp.zeros((count,), jnp.int32).at[ranking[jnp.where(places < fixed, places, passed)]].set(jnp.asarray(lengths, jnp.int32))

    lengths = jnp.where(number % 4 == 0, named(crowded, number // 4), named(common, number - number // 4 - 1))
    mixed = jax.random.permutation(jax.random.fold_in(own, 3), count)
    donor, sink = mixed[0:count // 2 * 2:2], mixed[1:count // 2 * 2:2]
    slack = jnp.minimum(lengths[donor] - 1, limit - lengths[sink]) // 2
    slack = jnp.where((donor == ranking[0]) | (sink == ranking[0]) | (lengths[sink] == 0), 0, jnp.maximum(slack, 0))
    passed = jax.random.randint(jax.random.fold_in(own, 4), (count // 2,), 0, 1 << 20) % (slack + 1)
    lengths = lengths.at[donor].add(-passed).at[sink].add(passed)
    items = jnp.searchsorted(jnp.cumsum(lengths), jnp.arange(rows * top), side="right").astype(jnp.int32)
    listing = items.reshape(top, rows).T
    listing = listing[jax.random.permutation(jax.random.fold_in(own, 1), rows)]
    rotation = jax.random.randint(jax.random.fold_in(own, 2), (rows, 1), 0, top)
    return jnp.take_along_axis(listing, (jnp.arange(top)[None, :] + rotation) % top, axis=1)


def portions_of(count, total, reach, lean, full):
    weights = [(1 << 20) // math.isqrt(grade ** lean) + 1 for grade in range(1, count + 1)]
    largest = reach if full else min(reach, max(-(-total // count), total * weights[0] // sum(weights)))
    least = 1 if total - largest >= count - 1 else 0
    given, surplus = [largest] + [least] * (count - 1), total - largest - least * (count - 1)
    while surplus > 0:
        free = [i for i in range(1, count) if given[i] < largest] or [i for i in range(1, count) if given[i] < reach]
        mass, left = sum([weights[i] for i in free]), surplus
        for i in free:
            addition = min(reach - given[i], max(1, left * weights[i] // mass), surplus)
            given[i] = given[i] + addition
            surplus = surplus - addition
    return np.array(given)


def gaussian(stream_key, shape, width, bound, pieces=(), held_as=jnp.bfloat16):
    loudness = block_scale(stream_key, shape, pieces, -0.22, 0.18) if pieces else 1.0
    entries = jax.random.normal(stream_key, shape, jnp.float32) * width * loudness
    return jnp.minimum(jnp.maximum(entries, -bound), bound).astype(held_as)


def setup_inputs(seed: int = 0) -> dict:
    arg_keys = jax.random.split(jax.random.key(seed), 6)
    air_state = gaussian(arg_keys[0], (COLUMNS, FEAT), 1.0, 6.0, ((0, 512),))
    owner_map_keys = jax.random.split(jax.random.fold_in(arg_keys[1], 1), COLUMNS // COLS_DEV)
    owner_map_turns = jax.random.permutation(jax.random.fold_in(arg_keys[1], 3), COLUMNS // COLS_DEV)
    owner_map = jax.vmap(lambda own, number: shared_out(jax.random.fold_in(arg_keys[1], 2), own, number, COLS_DEV, N_ROW, 1, CAP, 2))(owner_map_keys, owner_map_turns).reshape((COLUMNS, 1))
    cost_class = set_ends(jax.random.randint(arg_keys[2], (COLUMNS,), 0, NCLASS), jax.random.fold_in(arg_keys[2], 1), 0, NCLASS - 1).astype(jnp.int32)
    connectivity = draw_connectivity(jax.random.fold_in(arg_keys[5], 71), 0)
    inverse_blocks = gaussian(arg_keys[4], (OWNERS, NCLASS, 3, LEV, LEV), LEV ** -0.5, 0.5, ((0, 512),))
    return dict(air_state=air_state, owner_map=owner_map, cost_class=cost_class, connectivity=connectivity, inverse_blocks=inverse_blocks)


viscosity = 0.25


def apply_blocks(air_state, owner_map, cost_class, inverse_blocks):
    column_total = air_state.shape[0]
    position = jnp.arange(column_total, dtype=jnp.int32)
    owners = owner_map[:, 0] * N_COL + (position // COLS_DEV) % N_COL
    op_index = (owners * NCLASS + cost_class).astype(jnp.int32)
    all_blocks = inverse_blocks.reshape(OWNERS * NCLASS, 3, LEV, LEV)
    block_size = min(256, COLS_DEV)
    block_count = column_total // block_size

    def one_block(pair):
        row_block, block_picks = pair
        blocks = all_blocks[block_picks].astype(jnp.float32)
        fields = row_block.reshape(block_size, 3, LEV).astype(jnp.float32)
        result = jnp.einsum("nfm,nflm->nfl", fields, blocks)
        return result.reshape(block_size, FEAT).astype(jnp.bfloat16)

    physics = lax.map(one_block, (air_state.reshape(block_count, block_size, FEAT), op_index.reshape(block_count, block_size)))
    return physics.reshape(column_total, FEAT)


def edge_sums(air_state, connectivity):
    grouped = air_state.astype(jnp.float32).reshape(N_ROW, GROUP_COLS, FEAT)
    offsets = connectivity.reshape(PARTNERS, N_ROW, GROUP_COLS)
    places = jnp.arange(GROUP_COLS, dtype=jnp.int32)[None, :]
    laplace_sum = jnp.zeros_like(grouped)
    for partner in range(PARTNERS):
        target = ((places + offsets[partner]) % GROUP_COLS).astype(jnp.int32)
        gathered = jax.vmap(lambda source_table, row_picks: source_table[row_picks])(grouped, target)
        laplace_sum = laplace_sum + (gathered - grouped)
    return laplace_sum.reshape(N_ROW * GROUP_COLS, FEAT)


def reference(air_state, owner_map, cost_class, connectivity, inverse_blocks):
    physics = apply_blocks(air_state, owner_map, cost_class, inverse_blocks)
    laplace_sum = edge_sums(air_state, connectivity)
    return (physics.astype(jnp.float32) + viscosity * laplace_sum).astype(jnp.bfloat16)
```

```python
import math

import jax
import jax.numpy as jnp
from jax import lax
from jax.sharding import PartitionSpec as P

viscosity = 0.25


def padded(cells, sides, width):
    for axis, dim in sides:
        count = lax.axis_size(axis)
        head = lax.slice_in_dim(cells, 0, width, axis=dim)
        tail = lax.slice_in_dim(cells, cells.shape[dim] - width, cells.shape[dim], axis=dim)
        cells = jnp.concatenate(
            [
                lax.ppermute(tail, axis, [(i, (i + 1) % count) for i in range(count)]),
                cells,
                lax.ppermute(head, axis, [((i + 1) % count, i) for i in range(count)]),
            ],
            axis=dim,
        )
    return cells


def apply_local(received, labels_in, inverse_blocks):
    layout_shape = received.shape
    levels = inverse_blocks.shape[-1]
    classes = inverse_blocks.shape[1]
    slot_total = layout_shape[0] * layout_shape[1]
    fields = received.reshape(slot_total, 3, levels)
    labels = labels_in.reshape(slot_total)
    block_rows = math.gcd(256, slot_total)
    class_values = jnp.arange(classes, dtype=jnp.int32).astype(jnp.bfloat16)
    own_blocks = inverse_blocks[0]

    def one_block(pair):
        field_block, label_block = pair
        selector = (label_block[:, None] == class_values[None, :]).astype(jnp.bfloat16)
        spread = field_block[:, None, :, :] * selector[:, :, None, None]
        result = jnp.einsum(
            "rcfm,cflm->rfl", spread, own_blocks, preferred_element_type=jnp.float32
        )
        return result.astype(jnp.bfloat16)

    computed = lax.map(
        one_block, (fields.reshape(-1, block_rows, 3, levels), labels.reshape(-1, block_rows))
    )
    return computed.reshape(layout_shape)


def pack_slots(air_state, targets, slot_index, cost_class, groups, capacity):
    outgoing = (
        jnp.zeros((groups, capacity, air_state.shape[1]), jnp.bfloat16)
        .at[targets, slot_index]
        .set(air_state)
    )
    labels_out = (
        jnp.full((groups, capacity), -1.0, jnp.bfloat16)
        .at[targets, slot_index]
        .set(cost_class.astype(jnp.bfloat16))
    )
    return (outgoing, labels_out)


def per_device(air_state, owner_map, cost_class, connectivity, inverse_blocks):
    groups = lax.axis_size("row")
    local_count = air_state.shape[0]
    capacity = 2 * local_count // groups
    targets = owner_map[:, 0]
    earlier = jnp.arange(local_count)[:, None] > jnp.arange(local_count)[None, :]
    same = targets[:, None] == targets[None, :]
    slot_index = jnp.sum((earlier & same).astype(jnp.int32), axis=1)
    halo_width = local_count // 4
    extended = padded(air_state, (("col", 0),), halo_width)
    center = air_state.astype(jnp.float32)
    places = jnp.arange(local_count, dtype=jnp.int32) + halo_width
    laplace_sum = jnp.zeros_like(center)
    for partner in range(connectivity.shape[0]):
        laplace_sum = laplace_sum + (
            extended[places + connectivity[partner]].astype(jnp.float32) - center
        )
    outgoing, labels_out = pack_slots(air_state, targets, slot_index, cost_class, groups, capacity)
    received, labels_in = (
        lax.all_to_all(outgoing, "row", split_axis=0, concat_axis=0, tiled=True),
        lax.all_to_all(labels_out, "row", split_axis=0, concat_axis=0, tiled=True),
    )
    computed = apply_local(received, labels_in, inverse_blocks)
    returned = lax.all_to_all(computed, "row", split_axis=0, concat_axis=0, tiled=True)
    physics = returned[targets, slot_index]
    return (physics.astype(jnp.float32) + viscosity * laplace_sum).astype(jnp.bfloat16)


def solution(mesh):
    return jax.shard_map(
        per_device,
        mesh=mesh,
        in_specs=(
            P(("row", "col"), None),
            P(("row", "col"), None),
            P(("row", "col")),
            P(None, ("row", "col")),
            P(("row", "col"), None, None, None, None),
        ),
        out_specs=P(("row", "col"), None),
        check_vma=False,
    )
```

```python
import functools

import jax
import jax.numpy as jnp
from jax import lax
from jax.experimental import pallas as pl
from jax.experimental.pallas import tpu as pltpu
from jax.sharding import PartitionSpec as P

MESH = pl.DeviceIdType.MESH
F32 = jnp.float32
BF16 = jnp.bfloat16
viscosity = 0.25


def kernel(sizes, air, owner, cost, conn, blocks, out, ext, owner_v, cost_v, conn_v, blocks_v, pick, pick_t, wt, send,
           recv, back, home, load_sem, halo_send, halo_recv, send_sem, recv_sem, back_send, back_recv):
    rows, cols, cap, halo, groups = sizes
    row, col = lax.axis_index("row"), lax.axis_index("col")
    left, right = lax.rem(col + cols - 1, cols), lax.rem(col + 1, cols)
    local, feat = air.shape
    classes, fields, levels = blocks_v.shape[:3]
    slots = rows * cap

    barrier = pltpu.get_barrier_semaphore()

    def greet(i, carry):
        pl.semaphore_signal(barrier, inc=1, device_id=(row ^ (rows - 1 - i), col), device_id_type=MESH)
        return carry

    lax.fori_loop(0, rows - 1, greet, 0)
    for side in (left, right):
        pl.semaphore_signal(barrier, inc=1, device_id=(row, side), device_id_type=MESH)

    center = ext.at[pl.ds(halo, local)]
    loads = [
        pltpu.make_async_copy(src, dst, load_sem.at[i])
        for i, (src, dst) in enumerate(
            ((owner, owner_v), (cost, cost_v), (air, center), (conn, conn_v), (blocks, blocks_v))
        )
    ]
    for load in loads:
        load.start()

    loads[0].wait()
    target = jnp.broadcast_to(owner_v[...], (local, local)).astype(F32)
    sub = lax.broadcasted_iota(jnp.int32, (local, local), 0)
    lane = lax.broadcasted_iota(jnp.int32, (local, local), 1)
    same = jnp.where((target == target.T) & (sub < lane), 1.0, 0.0)
    rank = jnp.sum(same, axis=0, keepdims=True).astype(jnp.int32)
    key = (owner_v[...] ^ row) * cap + rank
    slot_id = lax.broadcasted_iota(jnp.int32, (slots, local), 0)
    hit = jnp.where(slot_id == key, 1.0, 0.0)
    loads[1].wait()
    label = jnp.sum(hit * cost_v[...].astype(F32), axis=1, keepdims=True)
    pick[...] = hit.astype(BF16)
    loads[2].wait()
    packed = jnp.dot(pick[...], ext[pl.ds(halo, local), :], preferred_element_type=F32)
    packed = jnp.concatenate([packed, jnp.broadcast_to(label, (slots, levels))], axis=1)
    send[...] = packed.reshape(rows, cap, feat + levels).astype(BF16)

    pl.semaphore_wait(barrier, rows + 1)

    def forward(group):
        low, high = groups[group]

        def one(i, carry):
            j = high - 1 - i
            pltpu.make_async_remote_copy(
                send.at[j], recv.at[j], send_sem, recv_sem.at[group], device_id=(row ^ j, col), device_id_type=MESH
            ).start()
            return carry

        lax.fori_loop(0, high - max(low, 1), one, 0)

    halos = [
        pltpu.make_async_remote_copy(
            ext.at[pl.ds(local, halo)], ext.at[pl.ds(0, halo)], halo_send.at[0], halo_recv.at[0],
            device_id=(row, right), device_id_type=MESH,
        ),
        pltpu.make_async_remote_copy(
            ext.at[pl.ds(halo, halo)], ext.at[pl.ds(halo + local, halo)], halo_send.at[1], halo_recv.at[1],
            device_id=(row, left), device_id_type=MESH,
        ),
    ]
    for group in range(len(groups)):
        forward(group)
        if group == 0:
            for copy in halos:
                copy.start()
    recv[0] = send[0]

    pick_t[...] = pick[...].T
    loads[4].wait()
    for f in range(fields):
        for c in range(classes):
            wt[f, pl.ds(c * levels, levels), :] = blocks_v[c, f].T
    loads[3].wait()

    def laplace():
        for copy in halos:
            copy.wait()
        place = lax.broadcasted_iota(jnp.int32, (local + 2 * halo, local), 0)
        spot = lax.broadcasted_iota(jnp.int32, (1, local), 1) + halo
        count = jnp.where(place == spot, -float(conn_v.shape[0]), 0.0)
        for k in range(conn_v.shape[0]):
            count += jnp.where(place == spot + conn_v[pl.ds(k, 1), :], 1.0, 0.0)
        out[...] = viscosity * jnp.dot(count.T.astype(BF16), ext[...], preferred_element_type=F32)

    def wait_for(buffer, sem, number):
        part = buffer.at[pl.ds(0, number)]
        pltpu.make_async_copy(part, part, sem).wait()

    def work(group):
        low, high = groups[group]
        number = high - low
        wait_for(recv, recv_sem.at[group], high - max(low, 1))
        block = recv[pl.ds(low, number)].astype(F32).reshape(number * cap, feat + levels)
        tag = block[:, feat:]
        made = []
        for f in range(fields):
            part = block[:, f * levels : (f + 1) * levels]
            spread = jnp.concatenate([jnp.where(tag == float(c), part, 0.0).astype(BF16) for c in range(classes)], axis=1)
            made.append(jnp.dot(spread, wt[f], preferred_element_type=F32))
        back[pl.ds(low, number)] = jnp.concatenate(made, axis=1).reshape(number, cap, feat).astype(BF16)

        def one(i, carry):
            j = high - 1 - i
            pltpu.make_async_remote_copy(
                back.at[j], home.at[j], back_send, back_recv, device_id=(row ^ j, col), device_id_type=MESH
            ).start()
            return carry

        lax.fori_loop(0, high - max(low, 1), one, 0)
        if low == 0:
            home[0] = back[0]

    near = len(groups) - 1
    work(near)
    laplace()
    for group in range(near):
        work(group)
    wait_for(home, back_recv, rows - 1)
    returned = home[...].astype(F32).reshape(slots, feat).astype(BF16)
    out[...] += jnp.dot(pick_t[...], returned, preferred_element_type=F32)
    wait_for(send, send_sem, rows - 1)
    wait_for(back, back_send, rows - 1)


def per_device(rows, cols, air, owner, cost, conn, blocks):
    local, feat = air.shape
    classes, fields, levels = blocks.shape[1:4]
    halo = local // 4
    cap = 2 * local // rows
    slots = rows * cap
    step = rows // 8
    groups = tuple((low, low + step) for low in range(rows - step, rows // 2 - 1, -step)) + ((0, rows // 2),)
    n = len(groups)
    sizes = (rows, cols, cap, halo, groups)
    total = pl.pallas_call(
        functools.partial(kernel, sizes),
        out_shape=jax.ShapeDtypeStruct((local, feat), F32),
        in_specs=[pl.BlockSpec(memory_space=pl.ANY)] * 5,
        out_specs=pl.BlockSpec(memory_space=pltpu.VMEM),
        scratch_shapes=[
            pltpu.VMEM((local + 2 * halo, feat), BF16),
            pltpu.VMEM((1, local), jnp.int32),
            pltpu.VMEM((1, local), jnp.int32),
            pltpu.VMEM(conn.shape, jnp.int32),
            pltpu.VMEM((classes, fields, levels, levels), BF16),
            pltpu.VMEM((slots, local), BF16),
            pltpu.VMEM((local, slots), BF16),
            pltpu.VMEM((fields, classes * levels, levels), BF16),
            pltpu.VMEM((rows, cap, feat + levels), BF16),
            pltpu.VMEM((rows, cap, feat + levels), BF16),
            pltpu.VMEM((rows, cap, feat), BF16),
            pltpu.VMEM((rows, cap, feat), BF16),
            pltpu.SemaphoreType.DMA((5,)),
            pltpu.SemaphoreType.DMA((2,)),
            pltpu.SemaphoreType.DMA((2,)),
            pltpu.SemaphoreType.DMA,
            pltpu.SemaphoreType.DMA((n,)),
            pltpu.SemaphoreType.DMA,
            pltpu.SemaphoreType.DMA,
        ],
        compiler_params=pltpu.CompilerParams(collective_id=0, has_side_effects=True),
    )(air, owner.reshape(1, local), cost.reshape(1, local), conn, blocks.reshape(blocks.shape[1:]))
    return total.astype(BF16)


def solution(mesh):
    return jax.shard_map(
        functools.partial(per_device, mesh.shape["row"], mesh.shape["col"]),
        mesh=mesh,
        in_specs=(
            P(("row", "col"), None),
            P(("row", "col"), None),
            P(("row", "col")),
            P(None, ("row", "col")),
            P(("row", "col"), None, None, None, None),
        ),
        out_specs=P(("row", "col"), None),
        check_vma=False,
    )
```

```python
import functools

import jax
import jax.numpy as jnp
from jax import lax
from jax.experimental import pallas as pl
from jax.experimental.pallas import tpu as pltpu
from jax.sharding import PartitionSpec as P

MESH = pl.DeviceIdType.MESH
F32 = jnp.float32
BF16 = jnp.bfloat16
viscosity = 0.25


def kernel(sizes, air, owner, cost, conn, blocks, out, ext, owner_v, cost_v, conn_v, blocks_v, pick, pick_t, wt, send,
           recv, back, home, tag_out, tag_in, tags, far_tag, load_sem, halo_send, halo_recv, far_send, near_send, recv_sem,
           tag_send, tag_recv, pass_send, pass_recv, back_send, back_recv):
    rows, cols, cap, halo, groups = sizes
    row, col = lax.axis_index("row"), lax.axis_index("col")
    left, right = lax.rem(col + cols - 1, cols), lax.rem(col + 1, cols)
    local, feat = air.shape
    classes, fields, levels = blocks_v.shape[:3]
    slots, half = rows * cap, rows // 2
    near = len(groups) - 1

    barrier = pltpu.get_barrier_semaphore()

    def greet(i, carry):
        pl.semaphore_signal(barrier, inc=1, device_id=(row ^ (rows - 1 - i), col), device_id_type=MESH)
        return carry

    lax.fori_loop(0, rows - 1, greet, 0)
    for side in (left, right):
        pl.semaphore_signal(barrier, inc=1, device_id=(row, side), device_id_type=MESH)

    center = ext.at[pl.ds(halo, local)]
    loads = [
        pltpu.make_async_copy(src, dst, load_sem.at[i])
        for i, (src, dst) in enumerate(
            ((owner, owner_v), (cost, cost_v), (air, center), (conn, conn_v), (blocks, blocks_v))
        )
    ]
    for load in loads:
        load.start()

    loads[0].wait()
    target = jnp.broadcast_to(owner_v[...], (local, local)).astype(F32)
    sub = lax.broadcasted_iota(jnp.int32, (local, local), 0)
    lane = lax.broadcasted_iota(jnp.int32, (local, local), 1)
    same = jnp.where((target == target.T) & (sub < lane), 1.0, 0.0)
    rank = jnp.sum(same, axis=0, keepdims=True).astype(jnp.int32)
    key = (owner_v[...] ^ row) * cap + rank
    slot_id = lax.broadcasted_iota(jnp.int32, (slots, local), 0)
    hit = jnp.where(slot_id == key, 1.0, 0.0)
    loads[1].wait()
    label = jnp.sum(hit * cost_v[...].astype(F32), axis=1, keepdims=True)
    pick[...] = hit.astype(BF16)
    loads[2].wait()
    packed = jnp.dot(pick[...], ext[pl.ds(halo, local), :], preferred_element_type=F32)
    classes_row = jnp.broadcast_to(cost_v[...].astype(F32), (8, local)).astype(BF16)
    tag_row = lax.dot_general(classes_row, pick[pl.ds(half * cap, half * cap), :], (((1,), (1,)), ((), ())), preferred_element_type=F32)
    tag_out[...] = tag_row[:1]
    packed = jnp.concatenate([packed, jnp.broadcast_to(label, (slots, levels))], axis=1)
    send[...] = packed.reshape(rows, cap, feat + levels).astype(BF16)

    pl.semaphore_wait(barrier, rows + 1)

    tag_copy = pltpu.make_async_remote_copy(
        tag_out, tag_in, tag_send, tag_recv, device_id=(row ^ half, col), device_id_type=MESH
    )

    def peers(low, high, copy):
        def one(i, carry):
            copy(high - 1 - i).start()
            return carry

        lax.fori_loop(0, high - max(low, 1), one, 0)

    def remote(src, dst, j, send_at, recv_at):
        return pltpu.make_async_remote_copy(src, dst, send_at, recv_at, device_id=(row ^ j, col), device_id_type=MESH)

    def forward(group):
        if group == near:
            peers(*groups[group], lambda j: remote(send.at[j], recv.at[j], j, near_send, recv_sem.at[group]))
        else:
            peers(*groups[group], lambda j: remote(
                send.at[j, :, pl.ds(0, feat)], recv.at[j, :, pl.ds(0, feat)], j, far_send, recv_sem.at[group]
            ))

    halos = [
        pltpu.make_async_remote_copy(
            ext.at[pl.ds(local, halo)], ext.at[pl.ds(0, halo)], halo_send.at[0], halo_recv.at[0],
            device_id=(row, right), device_id_type=MESH,
        ),
        pltpu.make_async_remote_copy(
            ext.at[pl.ds(halo, halo)], ext.at[pl.ds(halo + local, halo)], halo_send.at[1], halo_recv.at[1],
            device_id=(row, left), device_id_type=MESH,
        ),
    ]
    tag_copy.start()
    for group in range(len(groups)):
        forward(group)
        if group == 0:
            for copy in halos:
                copy.start()
    recv[0] = send[0]

    pick_t[...] = pick[...].T
    loads[4].wait()
    for f in range(fields):
        for c in range(classes):
            wt[f, pl.ds(c * levels, levels), :] = blocks_v[c, f].T
    loads[3].wait()

    def laplace():
        for copy in halos:
            copy.wait()
        place = lax.broadcasted_iota(jnp.int32, (local + 2 * halo, local), 0)
        spot = lax.broadcasted_iota(jnp.int32, (1, local), 1) + halo
        count = jnp.where(place == spot, -float(conn_v.shape[0]), 0.0)
        for k in range(conn_v.shape[0]):
            count += jnp.where(place == spot + conn_v[pl.ds(k, 1), :], 1.0, 0.0)
        out[...] = viscosity * jnp.dot(count.T.astype(BF16), ext[...], preferred_element_type=F32)

    def wait_for(part, sem):
        pltpu.make_async_copy(part, part, sem).wait()

    def work(group):
        low, high = groups[group]
        number = high - low
        if group == near:
            wait_for(recv.at[pl.ds(1, number - 1)], recv_sem.at[group])
            tag = recv[pl.ds(low, number), :, feat:].astype(F32).reshape(number * cap, levels)
        else:
            wait_for(recv.at[pl.ds(low, number), :, pl.ds(0, feat)], recv_sem.at[group])
            tag = far_tag[pl.ds((low - half) * cap, number * cap), :]
        block = recv[pl.ds(low, number), :, :feat].astype(F32).reshape(number * cap, feat)
        made = []
        for f in range(fields):
            part = block[:, f * levels : (f + 1) * levels]
            spread = jnp.concatenate([jnp.where(tag == float(c), part, 0.0).astype(BF16) for c in range(classes)], axis=1)
            made.append(jnp.dot(spread, wt[f], preferred_element_type=F32))
        back[pl.ds(low, number)] = jnp.concatenate(made, axis=1).reshape(number, cap, feat).astype(BF16)
        peers(low, high, lambda j: remote(back.at[j], home.at[j], j, back_send, back_recv))

    tag_copy.wait()
    peers(1, half, lambda j: remote(tag_in, tags.at[j], j, pass_send, pass_recv))
    tags[0] = tag_in[...]

    work(near)
    home[0] = back[0]
    laplace()

    wait_for(tags.at[pl.ds(1, half - 1)], pass_recv)
    rows_of = jnp.broadcast_to(tags[...], (half, cap, half * cap)).reshape(half * cap, half * cap)
    mine = lax.broadcasted_iota(jnp.int32, rows_of.shape, 0) == lax.broadcasted_iota(jnp.int32, rows_of.shape, 1)
    far_tag[...] = jnp.broadcast_to(jnp.sum(jnp.where(mine, rows_of, 0.0), axis=1, keepdims=True), (half * cap, levels))

    for group in range(near):
        work(group)
    wait_for(home.at[pl.ds(1, rows - 1)], back_recv)
    returned = home[...].astype(F32).reshape(slots, feat).astype(BF16)
    out[...] += jnp.dot(pick_t[...], returned, preferred_element_type=F32)
    wait_for(send.at[pl.ds(half, half), :, pl.ds(0, feat)], far_send)
    wait_for(send.at[pl.ds(1, half - 1)], near_send)
    wait_for(tags.at[pl.ds(1, half - 1)], pass_send)
    wait_for(back.at[pl.ds(1, rows - 1)], back_send)


def per_device(rows, cols, air, owner, cost, conn, blocks):
    local, feat = air.shape
    classes, fields, levels = blocks.shape[1:4]
    halo = local // 4
    cap = 2 * local // rows
    slots = rows * cap
    step = rows // 8
    groups = tuple((low, low + step) for low in range(rows - step, rows // 2 - 1, -step)) + ((0, rows // 2),)
    n = len(groups)
    sizes = (rows, cols, cap, halo, groups)
    total = pl.pallas_call(
        functools.partial(kernel, sizes),
        out_shape=pltpu.VMEM((local, feat), F32),
        in_specs=[pl.BlockSpec(memory_space=pl.ANY)] * 5,
        out_specs=pl.BlockSpec(memory_space=pltpu.VMEM),
        scratch_shapes=[
            pltpu.VMEM((local + 2 * halo, feat), BF16),
            pltpu.VMEM((1, local), jnp.int32),
            pltpu.VMEM((1, local), jnp.int32),
            pltpu.VMEM(conn.shape, jnp.int32),
            pltpu.VMEM((classes, fields, levels, levels), BF16),
            pltpu.VMEM((slots, local), BF16),
            pltpu.VMEM((local, slots), BF16),
            pltpu.VMEM((fields, classes * levels, levels), BF16),
            pltpu.VMEM((rows, cap, feat + levels), BF16),
            pltpu.VMEM((rows, cap, feat + levels), BF16),
            pltpu.VMEM((rows, cap, feat), BF16),
            pltpu.VMEM((rows, cap, feat), BF16),
            pltpu.VMEM((1, slots // 2), F32),
            pltpu.VMEM((1, slots // 2), F32),
            pltpu.VMEM((rows // 2, 1, slots // 2), F32),
            pltpu.VMEM((slots // 2, levels), F32),
            pltpu.SemaphoreType.DMA((5,)),
            pltpu.SemaphoreType.DMA((2,)),
            pltpu.SemaphoreType.DMA((2,)),
            pltpu.SemaphoreType.DMA,
            pltpu.SemaphoreType.DMA,
            pltpu.SemaphoreType.DMA((n,)),
            pltpu.SemaphoreType.DMA,
            pltpu.SemaphoreType.DMA,
            pltpu.SemaphoreType.DMA,
            pltpu.SemaphoreType.DMA,
            pltpu.SemaphoreType.DMA,
            pltpu.SemaphoreType.DMA,
        ],
        compiler_params=pltpu.CompilerParams(collective_id=0, has_side_effects=True),
    )(air, owner.reshape(1, local), cost.reshape(1, local), conn, blocks.reshape(blocks.shape[1:]))
    return total.astype(BF16)


def solution(mesh):
    return jax.shard_map(
        functools.partial(per_device, mesh.shape["row"], mesh.shape["col"]),
        mesh=mesh,
        in_specs=(
            P(("row", "col"), None),
            P(("row", "col"), None),
            P(("row", "col")),
            P(None, ("row", "col")),
            P(("row", "col"), None, None, None, None),
        ),
        out_specs=P(("row", "col"), None),
        check_vma=False,
    )
```

```python
import functools

import jax
import jax.numpy as jnp
from jax import lax
from jax.experimental import pallas as pl
from jax.experimental.pallas import tpu as pltpu
from jax.sharding import PartitionSpec as P

MESH = pl.DeviceIdType.MESH
F32 = jnp.float32
BF16 = jnp.bfloat16
viscosity = 0.25


def kernel(sizes, air, owner, cost, conn, blocks, out, ext, owner_v, cost_v, conn_v, blocks_v, pick, pick_t, wt, send,
           recv, back, home, tag_out, tag_in, tags, far_tag, load_sem, halo_send, halo_recv, far_send, near_send, recv_sem,
           tag_send, tag_recv, pass_send, pass_recv, back_send, back_recv):
    rows, cols, cap, halo, groups = sizes
    row, col = lax.axis_index("row"), lax.axis_index("col")
    left, right = lax.rem(col + cols - 1, cols), lax.rem(col + 1, cols)
    local, feat = air.shape
    classes, fields, levels = blocks_v.shape[:3]
    slots, half = rows * cap, rows // 2
    near = len(groups) - 1

    barrier = pltpu.get_barrier_semaphore()

    def greet(i, carry):
        pl.semaphore_signal(barrier, inc=1, device_id=(row ^ (rows - 1 - i), col), device_id_type=MESH)
        return carry

    lax.fori_loop(0, rows - 1, greet, 0)
    for side in (left, right):
        pl.semaphore_signal(barrier, inc=1, device_id=(row, side), device_id_type=MESH)

    center = ext.at[pl.ds(halo, local)]
    loads = [
        pltpu.make_async_copy(src, dst, load_sem.at[i])
        for i, (src, dst) in enumerate(
            ((owner, owner_v), (cost, cost_v), (air, center), (conn, conn_v), (blocks, blocks_v))
        )
    ]
    for load in loads:
        load.start()

    loads[0].wait()
    target = jnp.broadcast_to(owner_v[...], (local, local)).astype(F32)
    sub = lax.broadcasted_iota(jnp.int32, (local, local), 0)
    lane = lax.broadcasted_iota(jnp.int32, (local, local), 1)
    same = jnp.where((target == target.T) & (sub < lane), 1.0, 0.0)
    rank = jnp.sum(same, axis=0, keepdims=True).astype(jnp.int32)
    key = (owner_v[...] ^ row) * cap + rank
    slot_id = lax.broadcasted_iota(jnp.int32, (slots, local), 0)
    hit = jnp.where(slot_id == key, 1.0, 0.0)
    loads[1].wait()
    label = jnp.sum(hit * cost_v[...].astype(F32), axis=1, keepdims=True)
    pick[...] = hit.astype(BF16)
    loads[2].wait()
    packed = jnp.dot(pick[...], ext[pl.ds(halo, local), :], preferred_element_type=F32)
    classes_row = jnp.broadcast_to(cost_v[...].astype(F32), (8, local)).astype(BF16)
    tag_row = lax.dot_general(classes_row, pick[pl.ds(half * cap, half * cap), :], (((1,), (1,)), ((), ())), preferred_element_type=F32)
    tag_out[...] = tag_row[:1]
    packed = jnp.concatenate([packed, jnp.broadcast_to(label, (slots, levels))], axis=1)
    send[...] = packed.reshape(rows, cap, feat + levels).astype(BF16)

    pl.semaphore_wait(barrier, rows + 1)

    tag_copy = pltpu.make_async_remote_copy(
        tag_out, tag_in, tag_send, tag_recv, device_id=(row ^ half, col), device_id_type=MESH
    )

    def peers(low, high, copy):
        def one(i, carry):
            copy(high - 1 - i).start()
            return carry

        lax.fori_loop(0, high - max(low, 1), one, 0)

    def remote(src, dst, j, send_at, recv_at):
        return pltpu.make_async_remote_copy(src, dst, send_at, recv_at, device_id=(row ^ j, col), device_id_type=MESH)

    def forward(group):
        if group == near:
            peers(*groups[group], lambda j: remote(send.at[j], recv.at[j], j, near_send, recv_sem.at[group]))
        else:
            peers(*groups[group], lambda j: remote(
                send.at[j, :, pl.ds(0, feat)], recv.at[j, :, pl.ds(0, feat)], j, far_send, recv_sem.at[group]
            ))

    halos = [
        pltpu.make_async_remote_copy(
            ext.at[pl.ds(local, halo)], ext.at[pl.ds(0, halo)], halo_send.at[0], halo_recv.at[0],
            device_id=(row, right), device_id_type=MESH,
        ),
        pltpu.make_async_remote_copy(
            ext.at[pl.ds(halo, halo)], ext.at[pl.ds(halo + local, halo)], halo_send.at[1], halo_recv.at[1],
            device_id=(row, left), device_id_type=MESH,
        ),
    ]
    def wait_for(part, sem):
        pltpu.make_async_copy(part, part, sem).wait()

    def turn():
        pick_t[...] = pick[...].T
        loads[4].wait()
        for f in range(fields):
            for c in range(classes):
                wt[f, pl.ds(c * levels, levels), :] = blocks_v[c, f].T
        loads[3].wait()


    first = col < 2
    held = (row >= half) & (col >= 2)
    tag_copy.start()
    for copy in halos:
        copy.start()

    @pl.when(first)
    def _():
        for group in range(near):
            forward(group)

    forward(near)

    @pl.when(jnp.logical_not(first))
    def _():
        for group in range(near):
            forward(group)

    turn()
    recv[0] = send[0]

    def laplace():
        for copy in halos:
            copy.wait()
        place = lax.broadcasted_iota(jnp.int32, (local + 2 * halo, local), 0)
        spot = lax.broadcasted_iota(jnp.int32, (1, local), 1) + halo
        count = jnp.where(place == spot, -float(conn_v.shape[0]), 0.0)
        for k in range(conn_v.shape[0]):
            count += jnp.where(place == spot + conn_v[pl.ds(k, 1), :], 1.0, 0.0)
        out[...] = viscosity * jnp.dot(count.T.astype(BF16), ext[...], preferred_element_type=F32)

    def arrived(group):
        low, high = groups[group]
        wait_for(recv.at[pl.ds(low, high - low), :, pl.ds(0, feat)], recv_sem.at[group])

    def work(group):
        low, high = groups[group]
        number = high - low
        if group == near:
            wait_for(recv.at[pl.ds(1, number - 1)], recv_sem.at[group])
            tag = recv[pl.ds(low, number), :, feat:].astype(F32).reshape(number * cap, levels)
        else:
            @pl.when(jnp.logical_not(held))
            def _():
                arrived(group)

            tag = far_tag[pl.ds((low - half) * cap, number * cap), :]
        block = recv[pl.ds(low, number), :, :feat].astype(F32).reshape(number * cap, feat)
        made = []
        for f in range(fields):
            part = block[:, f * levels : (f + 1) * levels]
            spread = jnp.concatenate([jnp.where(tag == float(c), part, 0.0).astype(BF16) for c in range(classes)], axis=1)
            made.append(jnp.dot(spread, wt[f], preferred_element_type=F32))
        back[pl.ds(low, number)] = jnp.concatenate(made, axis=1).reshape(number, cap, feat).astype(BF16)
        peers(low, high, lambda j: remote(back.at[j], home.at[j], j, back_send, back_recv))

    tag_copy.wait()
    peers(1, half, lambda j: remote(tag_in, tags.at[j], j, pass_send, pass_recv))
    tags[0] = tag_in[...]

    work(near)
    home[0] = back[0]
    laplace()

    wait_for(tags.at[pl.ds(1, half - 1)], pass_recv)
    rows_of = jnp.broadcast_to(tags[...], (half, cap, half * cap)).reshape(half * cap, half * cap)
    mine = lax.broadcasted_iota(jnp.int32, rows_of.shape, 0) == lax.broadcasted_iota(jnp.int32, rows_of.shape, 1)
    far_tag[...] = jnp.broadcast_to(jnp.sum(jnp.where(mine, rows_of, 0.0), axis=1, keepdims=True), (half * cap, levels))

    @pl.when(held)
    def _():
        for group in range(near):
            arrived(group)

    for group in range(near):
        work(group)
    wait_for(home.at[pl.ds(1, rows - 1)], back_recv)
    returned = home[...].astype(F32).reshape(slots, feat).astype(BF16)
    out[...] += jnp.dot(pick_t[...], returned, preferred_element_type=F32)
    wait_for(send.at[pl.ds(half, half), :, pl.ds(0, feat)], far_send)
    wait_for(send.at[pl.ds(1, half - 1)], near_send)
    wait_for(tags.at[pl.ds(1, half - 1)], pass_send)
    wait_for(back.at[pl.ds(1, rows - 1)], back_send)


def per_device(rows, cols, air, owner, cost, conn, blocks):
    local, feat = air.shape
    classes, fields, levels = blocks.shape[1:4]
    halo = local // 4
    cap = 2 * local // rows
    slots = rows * cap
    step = rows // 8
    groups = tuple((low, low + step) for low in range(rows - step, rows // 2 - 1, -step)) + ((0, rows // 2),)
    n = len(groups)
    sizes = (rows, cols, cap, halo, groups)
    total = pl.pallas_call(
        functools.partial(kernel, sizes),
        out_shape=pltpu.VMEM((local, feat), F32),
        in_specs=[pl.BlockSpec(memory_space=pl.ANY)] * 5,
        out_specs=pl.BlockSpec(memory_space=pltpu.VMEM),
        scratch_shapes=[
            pltpu.VMEM((local + 2 * halo, feat), BF16),
            pltpu.VMEM((1, local), jnp.int32),
            pltpu.VMEM((1, local), jnp.int32),
            pltpu.VMEM(conn.shape, jnp.int32),
            pltpu.VMEM((classes, fields, levels, levels), BF16),
            pltpu.VMEM((slots, local), BF16),
            pltpu.VMEM((local, slots), BF16),
            pltpu.VMEM((fields, classes * levels, levels), BF16),
            pltpu.VMEM((rows, cap, feat + levels), BF16),
            pltpu.VMEM((rows, cap, feat + levels), BF16),
            pltpu.VMEM((rows, cap, feat), BF16),
            pltpu.VMEM((rows, cap, feat), BF16),
            pltpu.VMEM((1, slots // 2), F32),
            pltpu.VMEM((1, slots // 2), F32),
            pltpu.VMEM((rows // 2, 1, slots // 2), F32),
            pltpu.VMEM((slots // 2, levels), F32),
            pltpu.SemaphoreType.DMA((5,)),
            pltpu.SemaphoreType.DMA((2,)),
            pltpu.SemaphoreType.DMA((2,)),
            pltpu.SemaphoreType.DMA,
            pltpu.SemaphoreType.DMA,
            pltpu.SemaphoreType.DMA((n,)),
            pltpu.SemaphoreType.DMA,
            pltpu.SemaphoreType.DMA,
            pltpu.SemaphoreType.DMA,
            pltpu.SemaphoreType.DMA,
            pltpu.SemaphoreType.DMA,
            pltpu.SemaphoreType.DMA,
        ],
        compiler_params=pltpu.CompilerParams(collective_id=0, has_side_effects=True),
    )(air, owner.reshape(1, local), cost.reshape(1, local), conn, blocks.reshape(blocks.shape[1:]))
    return total.astype(BF16)


def solution(mesh):
    return jax.shard_map(
        functools.partial(per_device, mesh.shape["row"], mesh.shape["col"]),
        mesh=mesh,
        in_specs=(
            P(("row", "col"), None),
            P(("row", "col"), None),
            P(("row", "col")),
            P(None, ("row", "col")),
            P(("row", "col"), None, None, None, None),
        ),
        out_specs=P(("row", "col"), None),
        check_vma=False,
    )
```

```python
import functools

import jax
import jax.numpy as jnp
from jax import lax
from jax.experimental import pallas as pl
from jax.experimental.pallas import tpu as pltpu
from jax.sharding import PartitionSpec as P

MESH = pl.DeviceIdType.MESH
F32 = jnp.float32
BF16 = jnp.bfloat16
viscosity = 0.25


def kernel(sizes, air, owner, cost, conn, blocks, out, ext, owner_v, cost_v, conn_v, blocks_v, pick, pick_t, wt, send,
           recv, back, home, tag_out, tag_in, tags, far_tag, load_sem, halo_send, halo_recv, far_send, near_send, recv_sem,
           tag_send, tag_recv, pass_send, pass_recv, back_send, back_recv):
    rows, cols, cap, halo, groups = sizes
    row, col = lax.axis_index("row"), lax.axis_index("col")
    left, right = lax.rem(col + cols - 1, cols), lax.rem(col + 1, cols)
    local, feat = air.shape
    classes, fields, levels = blocks_v.shape[:3]
    slots, half = rows * cap, rows // 2
    near = len(groups) - 1

    barrier = pltpu.get_barrier_semaphore()

    def greet(i, carry):
        pl.semaphore_signal(barrier, inc=1, device_id=(row ^ (rows - 1 - i), col), device_id_type=MESH)
        return carry

    lax.fori_loop(0, rows - 1, greet, 0)
    for side in (left, right):
        pl.semaphore_signal(barrier, inc=1, device_id=(row, side), device_id_type=MESH)

    center = ext.at[pl.ds(halo, local)]
    loads = [
        pltpu.make_async_copy(src, dst, load_sem.at[i])
        for i, (src, dst) in enumerate(
            ((owner, owner_v), (cost, cost_v), (air, center), (conn, conn_v), (blocks, blocks_v))
        )
    ]
    for load in loads:
        load.start()

    loads[0].wait()
    target = jnp.broadcast_to(owner_v[...], (local, local)).astype(F32)
    sub = lax.broadcasted_iota(jnp.int32, (local, local), 0)
    lane = lax.broadcasted_iota(jnp.int32, (local, local), 1)
    same = jnp.where((target == target.T) & (sub < lane), 1.0, 0.0)
    rank = jnp.sum(same, axis=0, keepdims=True).astype(jnp.int32)
    key = (owner_v[...] ^ row) * cap + rank
    slot_id = lax.broadcasted_iota(jnp.int32, (slots, local), 0)
    hit = jnp.where(slot_id == key, 1.0, 0.0)
    loads[1].wait()
    label = jnp.sum(hit * cost_v[...].astype(F32), axis=1, keepdims=True)
    pick[...] = hit.astype(BF16)
    loads[2].wait()
    packed = jnp.dot(pick[...], ext[pl.ds(halo, local), :], preferred_element_type=F32)
    classes_row = jnp.broadcast_to(cost_v[...].astype(F32), (8, local)).astype(BF16)
    tag_row = lax.dot_general(classes_row, pick[pl.ds(half * cap, half * cap), :], (((1,), (1,)), ((), ())), preferred_element_type=F32)
    tag_out[...] = tag_row[:1]
    packed = jnp.concatenate([packed, jnp.broadcast_to(label, (slots, levels))], axis=1)
    send[...] = packed.reshape(rows, cap, feat + levels).astype(BF16)

    pl.semaphore_wait(barrier, rows + 1)

    tag_copy = pltpu.make_async_remote_copy(
        tag_out, tag_in, tag_send, tag_recv, device_id=(row ^ half, col), device_id_type=MESH
    )

    def peers(low, high, copy):
        def one(i, carry):
            copy(high - 1 - i).start()
            return carry

        lax.fori_loop(0, high - max(low, 1), one, 0)

    def remote(src, dst, j, send_at, recv_at):
        return pltpu.make_async_remote_copy(src, dst, send_at, recv_at, device_id=(row ^ j, col), device_id_type=MESH)

    def forward(group):
        if group == near:
            peers(*groups[group], lambda j: remote(send.at[j], recv.at[j], j, near_send, recv_sem.at[group]))
        else:
            peers(*groups[group], lambda j: remote(
                send.at[j, :, pl.ds(0, feat)], recv.at[j, :, pl.ds(0, feat)], j, far_send, recv_sem.at[group]
            ))

    halos = [
        pltpu.make_async_remote_copy(
            ext.at[pl.ds(local, halo)], ext.at[pl.ds(0, halo)], halo_send.at[0], halo_recv.at[0],
            device_id=(row, right), device_id_type=MESH,
        ),
        pltpu.make_async_remote_copy(
            ext.at[pl.ds(halo, halo)], ext.at[pl.ds(halo + local, halo)], halo_send.at[1], halo_recv.at[1],
            device_id=(row, left), device_id_type=MESH,
        ),
    ]
    def wait_for(part, sem):
        pltpu.make_async_copy(part, part, sem).wait()

    def turn():
        pick_t[...] = pick[...].T
        loads[4].wait()
        for f in range(fields):
            for c in range(classes):
                wt[f, pl.ds(c * levels, levels), :] = blocks_v[c, f].T
        loads[3].wait()


    first = (col < 2) | (row >= half)
    held = (row >= half) & (col >= 2)
    tag_copy.start()
    for copy in halos:
        copy.start()

    @pl.when(first)
    def _():
        for group in range(near):
            forward(group)

    forward(near)

    @pl.when(jnp.logical_not(first))
    def _():
        turn()
        for group in range(near):
            forward(group)

    @pl.when(first)
    def _():
        turn()

    recv[0] = send[0]

    def laplace():
        for copy in halos:
            copy.wait()
        place = lax.broadcasted_iota(jnp.int32, (local + 2 * halo, local), 0)
        spot = lax.broadcasted_iota(jnp.int32, (1, local), 1) + halo
        count = jnp.where(place == spot, -float(conn_v.shape[0]), 0.0)
        for k in range(conn_v.shape[0]):
            count += jnp.where(place == spot + conn_v[pl.ds(k, 1), :], 1.0, 0.0)
        out[...] = viscosity * jnp.dot(count.T.astype(BF16), ext[...], preferred_element_type=F32)

    def arrived(group):
        low, high = groups[group]
        wait_for(recv.at[pl.ds(low, high - low), :, pl.ds(0, feat)], recv_sem.at[group])

    def work(group):
        low, high = groups[group]
        number = high - low
        if group == near:
            wait_for(recv.at[pl.ds(1, number - 1)], recv_sem.at[group])
            tag = recv[pl.ds(low, number), :, feat:].astype(F32).reshape(number * cap, levels)
        else:
            @pl.when(jnp.logical_not(held))
            def _():
                arrived(group)

            tag = far_tag[pl.ds((low - half) * cap, number * cap), :]
        block = recv[pl.ds(low, number), :, :feat].astype(F32).reshape(number * cap, feat)
        made = []
        for f in range(fields):
            part = block[:, f * levels : (f + 1) * levels]
            spread = jnp.concatenate([jnp.where(tag == float(c), part, 0.0).astype(BF16) for c in range(classes)], axis=1)
            made.append(jnp.dot(spread, wt[f], preferred_element_type=F32))
        back[pl.ds(low, number)] = jnp.concatenate(made, axis=1).reshape(number, cap, feat).astype(BF16)
        peers(low, high, lambda j: remote(back.at[j], home.at[j], j, back_send, back_recv))

    tag_copy.wait()
    peers(1, half, lambda j: remote(tag_in, tags.at[j], j, pass_send, pass_recv))
    tags[0] = tag_in[...]

    work(near)
    home[0] = back[0]
    laplace()

    wait_for(tags.at[pl.ds(1, half - 1)], pass_recv)
    rows_of = jnp.broadcast_to(tags[...], (half, cap, half * cap)).reshape(half * cap, half * cap)
    mine = lax.broadcasted_iota(jnp.int32, rows_of.shape, 0) == lax.broadcasted_iota(jnp.int32, rows_of.shape, 1)
    far_tag[...] = jnp.broadcast_to(jnp.sum(jnp.where(mine, rows_of, 0.0), axis=1, keepdims=True), (half * cap, levels))

    @pl.when(held)
    def _():
        for group in range(near):
            arrived(group)

    for group in range(near):
        work(group)
    wait_for(home.at[pl.ds(1, rows - 1)], back_recv)
    returned = home[...].astype(F32).reshape(slots, feat).astype(BF16)
    out[...] += jnp.dot(pick_t[...], returned, preferred_element_type=F32)
    wait_for(send.at[pl.ds(half, half), :, pl.ds(0, feat)], far_send)
    wait_for(send.at[pl.ds(1, half - 1)], near_send)
    wait_for(tags.at[pl.ds(1, half - 1)], pass_send)
    wait_for(back.at[pl.ds(1, rows - 1)], back_send)


def per_device(rows, cols, air, owner, cost, conn, blocks):
    local, feat = air.shape
    classes, fields, levels = blocks.shape[1:4]
    halo = local // 4
    cap = 2 * local // rows
    slots = rows * cap
    step = rows // 8
    groups = tuple((low, low + step) for low in range(rows - step, rows // 2 - 1, -step)) + ((0, rows // 2),)
    n = len(groups)
    sizes = (rows, cols, cap, halo, groups)
    total = pl.pallas_call(
        functools.partial(kernel, sizes),
        out_shape=pltpu.VMEM((local, feat), F32),
        in_specs=[pl.BlockSpec(memory_space=pl.ANY)] * 5,
        out_specs=pl.BlockSpec(memory_space=pltpu.VMEM),
        scratch_shapes=[
            pltpu.VMEM((local + 2 * halo, feat), BF16),
            pltpu.VMEM((1, local), jnp.int32),
            pltpu.VMEM((1, local), jnp.int32),
            pltpu.VMEM(conn.shape, jnp.int32),
            pltpu.VMEM((classes, fields, levels, levels), BF16),
            pltpu.VMEM((slots, local), BF16),
            pltpu.VMEM((local, slots), BF16),
            pltpu.VMEM((fields, classes * levels, levels), BF16),
            pltpu.VMEM((rows, cap, feat + levels), BF16),
            pltpu.VMEM((rows, cap, feat + levels), BF16),
            pltpu.VMEM((rows, cap, feat), BF16),
            pltpu.VMEM((rows, cap, feat), BF16),
            pltpu.VMEM((1, slots // 2), F32),
            pltpu.VMEM((1, slots // 2), F32),
            pltpu.VMEM((rows // 2, 1, slots // 2), F32),
            pltpu.VMEM((slots // 2, levels), F32),
            pltpu.SemaphoreType.DMA((5,)),
            pltpu.SemaphoreType.DMA((2,)),
            pltpu.SemaphoreType.DMA((2,)),
            pltpu.SemaphoreType.DMA,
            pltpu.SemaphoreType.DMA,
            pltpu.SemaphoreType.DMA((n,)),
            pltpu.SemaphoreType.DMA,
            pltpu.SemaphoreType.DMA,
            pltpu.SemaphoreType.DMA,
            pltpu.SemaphoreType.DMA,
            pltpu.SemaphoreType.DMA,
            pltpu.SemaphoreType.DMA,
        ],
        compiler_params=pltpu.CompilerParams(collective_id=0, has_side_effects=True),
    )(air, owner.reshape(1, local), cost.reshape(1, local), conn, blocks.reshape(blocks.shape[1:]))
    return total.astype(BF16)


def solution(mesh):
    return jax.shard_map(
        functools.partial(per_device, mesh.shape["row"], mesh.shape["col"]),
        mesh=mesh,
        in_specs=(
            P(("row", "col"), None),
            P(("row", "col"), None),
            P(("row", "col")),
            P(None, ("row", "col")),
            P(("row", "col"), None, None, None, None),
        ),
        out_specs=P(("row", "col"), None),
        check_vma=False,
    )
```

```python
import functools

import jax
import jax.numpy as jnp
from jax import lax
from jax.experimental import pallas as pl
from jax.experimental.pallas import tpu as pltpu
from jax.sharding import PartitionSpec as P

MESH = pl.DeviceIdType.MESH
F32 = jnp.float32
BF16 = jnp.bfloat16
viscosity = 0.25


def kernel(sizes, air, owner, cost, conn, blocks, out, ext, owner_v, cost_v, conn_v, blocks_v, pick, pick_t, wt, send,
           recv, back, home, tag_out, tag_in, tags, far_tag, load_sem, halo_send, halo_recv, far_send, near_send, recv_sem,
           tag_send, tag_recv, pass_send, pass_recv, back_send, back_recv):
    rows, cols, cap, halo, groups = sizes
    row, col = lax.axis_index("row"), lax.axis_index("col")
    left, right = lax.rem(col + cols - 1, cols), lax.rem(col + 1, cols)
    local, feat = air.shape
    classes, fields, levels = blocks_v.shape[:3]
    slots, half = rows * cap, rows // 2
    near = len(groups) - 1

    barrier = pltpu.get_barrier_semaphore()

    def greet(i, carry):
        pl.semaphore_signal(barrier, inc=1, device_id=(row ^ (rows - 1 - i), col), device_id_type=MESH)
        return carry

    lax.fori_loop(0, rows - 1, greet, 0)
    for side in (left, right):
        pl.semaphore_signal(barrier, inc=1, device_id=(row, side), device_id_type=MESH)

    center = ext.at[pl.ds(halo, local)]
    loads = [
        pltpu.make_async_copy(src, dst, load_sem.at[i])
        for i, (src, dst) in enumerate(
            ((owner, owner_v), (cost, cost_v), (air, center), (conn, conn_v), (blocks, blocks_v))
        )
    ]
    for load in loads:
        load.start()

    loads[0].wait()
    target = jnp.broadcast_to(owner_v[...], (local, local)).astype(F32)
    sub = lax.broadcasted_iota(jnp.int32, (local, local), 0)
    lane = lax.broadcasted_iota(jnp.int32, (local, local), 1)
    same = jnp.where((target == target.T) & (sub < lane), 1.0, 0.0)
    rank = jnp.sum(same, axis=0, keepdims=True).astype(jnp.int32)
    key = (owner_v[...] ^ row) * cap + rank
    slot_id = lax.broadcasted_iota(jnp.int32, (slots, local), 0)
    hit = jnp.where(slot_id == key, 1.0, 0.0)
    loads[1].wait()
    label = jnp.sum(hit * cost_v[...].astype(F32), axis=1, keepdims=True)
    pick[...] = hit.astype(BF16)
    loads[2].wait()
    packed = jnp.dot(pick[...], ext[pl.ds(halo, local), :], preferred_element_type=F32)
    classes_row = jnp.broadcast_to(cost_v[...].astype(F32), (8, local)).astype(BF16)
    tag_row = lax.dot_general(classes_row, pick[pl.ds(half * cap, half * cap), :], (((1,), (1,)), ((), ())), preferred_element_type=F32)
    tag_out[...] = tag_row[:1]
    packed = jnp.concatenate([packed, jnp.broadcast_to(label, (slots, levels))], axis=1)
    send[...] = packed.reshape(rows, cap, feat + levels).astype(BF16)

    pl.semaphore_wait(barrier, rows + 1)

    tag_copy = pltpu.make_async_remote_copy(
        tag_out, tag_in, tag_send, tag_recv, device_id=(row ^ half, col), device_id_type=MESH
    )

    def peers(low, high, copy):
        def one(i, carry):
            copy(high - 1 - i).start()
            return carry

        lax.fori_loop(0, high - max(low, 1), one, 0)

    def remote(src, dst, j, send_at, recv_at):
        return pltpu.make_async_remote_copy(src, dst, send_at, recv_at, device_id=(row ^ j, col), device_id_type=MESH)

    def forward(group):
        if group == near:
            peers(*groups[group], lambda j: remote(send.at[j], recv.at[j], j, near_send, recv_sem.at[group]))
        else:
            peers(*groups[group], lambda j: remote(
                send.at[j, :, pl.ds(0, feat)], recv.at[j, :, pl.ds(0, feat)], j, far_send, recv_sem.at[group]
            ))

    halos = [
        pltpu.make_async_remote_copy(
            ext.at[pl.ds(local, halo)], ext.at[pl.ds(0, halo)], halo_send.at[0], halo_recv.at[0],
            device_id=(row, right), device_id_type=MESH,
        ),
        pltpu.make_async_remote_copy(
            ext.at[pl.ds(halo, halo)], ext.at[pl.ds(halo + local, halo)], halo_send.at[1], halo_recv.at[1],
            device_id=(row, left), device_id_type=MESH,
        ),
    ]
    def wait_for(part, sem):
        pltpu.make_async_copy(part, part, sem).wait()

    def turn():
        pick_t[...] = pick[...].T
        loads[4].wait()
        for f in range(fields):
            for c in range(classes):
                wt[f, pl.ds(c * levels, levels), :] = blocks_v[c, f].T
        loads[3].wait()


    first = (col < 2) | (row >= half)
    held = (row >= half) & (col >= 2)
    tag_copy.start()
    for copy in halos:
        copy.start()

    @pl.when(first)
    def _():
        for group in range(near):
            forward(group)

    forward(near)

    @pl.when(jnp.logical_not(first))
    def _():
        turn()
        for group in range(near):
            forward(group)

    @pl.when(first)
    def _():
        turn()

    recv[0] = send[0]

    def laplace():
        for copy in halos:
            copy.wait()
        place = lax.broadcasted_iota(jnp.int32, (local + 2 * halo, local), 0)
        spot = lax.broadcasted_iota(jnp.int32, (1, local), 1) + halo
        count = jnp.where(place == spot, -float(conn_v.shape[0]), 0.0)
        for k in range(conn_v.shape[0]):
            count += jnp.where(place == spot + conn_v[pl.ds(k, 1), :], 1.0, 0.0)
        out[...] = viscosity * jnp.dot(count.T.astype(BF16), ext[...], preferred_element_type=F32)

    def arrived(group):
        low, high = groups[group]
        wait_for(recv.at[pl.ds(low, high - low), :, pl.ds(0, feat)], recv_sem.at[group])

    def work(group):
        low, high = groups[group]
        number = high - low
        if group == near:
            wait_for(recv.at[pl.ds(1, number - 1)], recv_sem.at[group])
            tag = recv[pl.ds(low, number), :, feat:].astype(F32).reshape(number * cap, levels)
        else:
            @pl.when(jnp.logical_not(held))
            def _():
                arrived(group)

            tag = far_tag[pl.ds((low - half) * cap, number * cap), :]
        block = recv[pl.ds(low, number), :, :feat].astype(F32).reshape(number * cap, feat)
        made = []
        for f in range(fields):
            part = block[:, f * levels : (f + 1) * levels]
            spread = jnp.concatenate([jnp.where(tag == float(c), part, 0.0).astype(BF16) for c in range(classes)], axis=1)
            made.append(jnp.dot(spread, wt[f], preferred_element_type=F32))
        back[pl.ds(low, number)] = jnp.concatenate(made, axis=1).reshape(number, cap, feat).astype(BF16)
        peers(low, high, lambda j: remote(back.at[j], home.at[j], j, back_send, back_recv))

    tag_copy.wait()
    peers(1, half, lambda j: remote(tag_in, tags.at[j], j, pass_send, pass_recv))
    tags[0] = tag_in[...]

    work(near)
    home[0] = back[0]
    laplace()

    wait_for(tags.at[pl.ds(1, half - 1)], pass_recv)
    rows_of = jnp.broadcast_to(tags[...], (half, cap, half * cap)).reshape(half * cap, half * cap)
    mine = lax.broadcasted_iota(jnp.int32, rows_of.shape, 0) == lax.broadcasted_iota(jnp.int32, rows_of.shape, 1)
    far_tag[...] = jnp.broadcast_to(jnp.sum(jnp.where(mine, rows_of, 0.0), axis=1, keepdims=True), (half * cap, levels))

    @pl.when(held)
    def _():
        for group in range(near):
            arrived(group)

    for group in range(near):
        work(group)
    wait_for(home.at[pl.ds(1, rows - 1)], back_recv)
    returned = home[...].astype(F32).reshape(slots, feat).astype(BF16)
    out[...] += jnp.dot(pick_t[...], returned, preferred_element_type=F32)
    wait_for(send.at[pl.ds(half, half), :, pl.ds(0, feat)], far_send)
    wait_for(send.at[pl.ds(1, half - 1)], near_send)
    wait_for(tags.at[pl.ds(1, half - 1)], pass_send)
    wait_for(back.at[pl.ds(1, rows - 1)], back_send)


def per_device(rows, cols, air, owner, cost, conn, blocks):
    local, feat = air.shape
    classes, fields, levels = blocks.shape[1:4]
    halo = local // 4
    cap = 2 * local // rows
    slots = rows * cap
    step = rows // 16
    groups = tuple((low, low + step) for low in range(rows - step, rows // 2 - 1, -step)) + ((0, rows // 2),)
    n = len(groups)
    sizes = (rows, cols, cap, halo, groups)
    total = pl.pallas_call(
        functools.partial(kernel, sizes),
        out_shape=pltpu.VMEM((local, feat), F32),
        in_specs=[pl.BlockSpec(memory_space=pl.ANY)] * 5,
        out_specs=pl.BlockSpec(memory_space=pltpu.VMEM),
        scratch_shapes=[
            pltpu.VMEM((local + 2 * halo, feat), BF16),
            pltpu.VMEM((1, local), jnp.int32),
            pltpu.VMEM((1, local), jnp.int32),
            pltpu.VMEM(conn.shape, jnp.int32),
            pltpu.VMEM((classes, fields, levels, levels), BF16),
            pltpu.VMEM((slots, local), BF16),
            pltpu.VMEM((local, slots), BF16),
            pltpu.VMEM((fields, classes * levels, levels), BF16),
            pltpu.VMEM((rows, cap, feat + levels), BF16),
            pltpu.VMEM((rows, cap, feat + levels), BF16),
            pltpu.VMEM((rows, cap, feat), BF16),
            pltpu.VMEM((rows, cap, feat), BF16),
            pltpu.VMEM((1, slots // 2), F32),
            pltpu.VMEM((1, slots // 2), F32),
            pltpu.VMEM((rows // 2, 1, slots // 2), F32),
            pltpu.VMEM((slots // 2, levels), F32),
            pltpu.SemaphoreType.DMA((5,)),
            pltpu.SemaphoreType.DMA((2,)),
            pltpu.SemaphoreType.DMA((2,)),
            pltpu.SemaphoreType.DMA,
            pltpu.SemaphoreType.DMA,
            pltpu.SemaphoreType.DMA((n,)),
            pltpu.SemaphoreType.DMA,
            pltpu.SemaphoreType.DMA,
            pltpu.SemaphoreType.DMA,
            pltpu.SemaphoreType.DMA,
            pltpu.SemaphoreType.DMA,
            pltpu.SemaphoreType.DMA,
        ],
        compiler_params=pltpu.CompilerParams(collective_id=0, has_side_effects=True),
    )(air, owner.reshape(1, local), cost.reshape(1, local), conn, blocks.reshape(blocks.shape[1:]))
    return total.astype(BF16)


def solution(mesh):
    return jax.shard_map(
        functools.partial(per_device, mesh.shape["row"], mesh.shape["col"]),
        mesh=mesh,
        in_specs=(
            P(("row", "col"), None),
            P(("row", "col"), None),
            P(("row", "col")),
            P(None, ("row", "col")),
            P(("row", "col"), None, None, None, None),
        ),
        out_specs=P(("row", "col"), None),
        check_vma=False,
    )
```
